768 devices in a mesh: grp: 16 (over y, core), rep: 48 (over x, z).
Axes of the slice: x: 4, y: 8, z: 12, core: 2. Of those that a mesh axis runs over, the one named last changes fastest.
Arguments:
- grad_part: float32 [16, 3072, 20, 512], P('grp', 'rep'), may hold values from -0.75 to 0.75
- owners: int32 [6, 20], replicated, may hold values from 0 to 47, as said below
- readers: int32 [48], replicated, may hold values from 0 to 47, each once
- left_stat: float32 [48, 4, 512, 512], P('rep', None, 'grp'), may hold values from -6 to 6
- right_stat: float32 [48, 4, 512, 512], P('rep', None, 'grp'), may hold values from -6 to 6
- left_root: bfloat16 [48, 4, 512, 512], P('rep'), may hold values from -1 to 2
- right_root: bfloat16 [48, 4, 512, 512], P('rep', None, None, 'grp'), may hold values from -1 to 2
Outputs:
- update: bfloat16 [3072, 20, 512], P('rep', None, 'grp')
- left_new: float32 [48, 4, 512, 512], P('rep', None, 'grp')
- right_new: float32 [48, 4, 512, 512], P('rep', None, 'grp')
The draws below stay inside these ranges and needn't reach their ends.
Inputs may be any that keep to these rules, and one draw needn't show every extreme that they name: `owners`: A device owns at most 1 block of one block row and at most 4 blocks in all; some device owns 4 blocks.
All inputs are finite; a program needn't handle non-finite values.
Results may differ from the reference program's by a relative error of at most 0.0057.
Values may be sent and summed in bfloat16 or wider, within the bound.
A program may use at most 64 MiB of HBM per device.

```python
import math
import jax
import jax.numpy as jnp
from jax import lax

BLOCK = 512
SHARD_ROWS = 64
ROWS = 3072
BLOCK_ROWS = 6
BLOCK_COLS = 20
SLOTS = 4
N_GRP = 16
N_REP = 48


def draw_owners(key, part):
    key = jax.random.fold_in(key, 11)
    key_heavy, key_perm, key_cols = jax.random.split(key, 3)
    block_total = BLOCK_ROWS * BLOCK_COLS
    heavy = 1 + jax.random.randint(key_heavy, (), 0, N_REP // 8 + 1)
    others = N_REP - heavy
    remainder = block_total - heavy * SLOTS
    base_load = remainder // others
    extra_load = remainder % others
    ranks = jnp.arange(N_REP, dtype=jnp.int32)
    loads = jnp.where(ranks < heavy, SLOTS, base_load + (ranks - heavy < extra_load).astype(jnp.int32))
    bounds = jnp.cumsum(loads)
    places = jnp.arange(block_total, dtype=jnp.int32)
    holder = jnp.sum((bounds[None, :] <= places[:, None]).astype(jnp.int32), axis=1)
    labels = jax.random.permutation(key_perm, N_REP).astype(jnp.int32)
    who = labels[holder]
    row_index = places % BLOCK_ROWS
    col_index = places // BLOCK_ROWS
    grid = jnp.zeros((BLOCK_ROWS, BLOCK_COLS), jnp.int32).at[row_index, col_index].set(who)
    row_keys = jax.random.split(key_cols, BLOCK_ROWS)
    shuffles = jax.vmap(lambda single: jax.random.permutation(single, BLOCK_COLS))(row_keys).astype(jnp.int32)
    row_ids = jnp.broadcast_to(jnp.arange(BLOCK_ROWS, dtype=jnp.int32)[:, None], (BLOCK_ROWS, BLOCK_COLS))
    return jnp.zeros((BLOCK_ROWS, BLOCK_COLS), jnp.int32).at[row_ids, shuffles].set(grid)


def build_root(noise, diagonal):
    paired = (noise + jnp.swapaxes(noise, -1, -2)) * (0.25 / math.sqrt(2.0 * BLOCK))
    identity = jnp.eye(BLOCK, dtype=jnp.float32)
    return paired + identity * diagonal[..., None]


def draw_left_root(key, part):
    key = jax.random.fold_in(key, 23)
    key_noise, key_diag = jax.random.split(key)
    shape = (N_REP, SLOTS, BLOCK, BLOCK)
    noise = jax.random.normal(key_noise, shape, jnp.float32)
    diagonal = jax.random.uniform(key_diag, shape[:-1], jnp.float32, 0.6, 1.4)
    return build_root(noise, diagonal).astype(jnp.bfloat16)


def draw_right_root(key, part):
    key = jax.random.fold_in(key, 37)
    key_noise, key_diag = jax.random.split(key)
    shape = (N_REP, SLOTS, BLOCK, BLOCK)
    noise = jax.random.normal(key_noise, shape, jnp.float32)
    diagonal = jax.random.uniform(key_diag, shape[:-1], jnp.float32, 0.6, 1.4)
    return build_root(noise, diagonal).astype(jnp.bfloat16)


def with_spikes(values, key, source, target, blocks, factor):
    def block_of(axis_at):
        return (jnp.arange(values.shape[axis_at]) // (values.shape[axis_at] // blocks)).reshape((-1,) + (1,) * (values.ndim - 1 - axis_at))

    first = jax.random.permutation(key, blocks)[block_of(target)]
    far = (block_of(target) + blocks // 2) % blocks
    return jnp.where((block_of(source) == first) | (block_of(source) == far), factor * values, values)


def level_of(rng, shape, cuts, least, top_value):
    def one(dim, blocks):
        draws = jax.random.uniform(jax.random.fold_in(jax.random.fold_in(rng, 6), dim), (blocks,), jnp.float32, least / len(cuts), top_value / len(cuts))
        return jnp.repeat(jnp.exp(draws), shape[dim] // blocks).reshape((-1,) + (1,) * (len(shape) - dim - 1))

    gain = one(*cuts[0])
    for cut in cuts[1:]:
        gain = gain * one(*cut)
    return gain


def bell_draw(stream_key, extent, width, limit, shards=(), held_as=jnp.bfloat16):
    values = width * jax.random.normal(stream_key, extent, jnp.float32)
    if shards:
        values = values * level_of(stream_key, extent, shards, -0.22, 0.18)
    return jnp.clip(values, -limit, limit).astype(held_as)


def heavy_noise(own_key, extent, width, most, pieces, heavy, kind=jnp.bfloat16):
    drawn = width * jax.random.normal(own_key, extent, jnp.float32)
    if pieces:
        drawn = drawn * level_of(own_key, extent, pieces, -0.22, 0.18)
    return jnp.clip(with_spikes(drawn, jax.random.fold_in(own_key, 3), *heavy), -most, most).astype(kind)


def setup_inputs(seed: int = 0) -> dict:
    key_of = jax.random.split(jax.random.key(seed), 8)
    grad_part = heavy_noise(key_of[0], (N_GRP, ROWS, BLOCK_COLS, BLOCK), 0.125, 0.75, ((0, 16), (1, 48)), (0, 3, 16, 2.0), jnp.float32)
    owners = draw_owners(jax.random.fold_in(key_of[7], 71), 0)
    readers = jax.random.permutation(key_of[2], N_REP).astype(jnp.int32)
    left_stat = bell_draw(key_of[3], (N_REP, SLOTS, BLOCK, BLOCK), 1.0, 6.0, ((0, 48), (2, 16)), jnp.float32)
    right_stat = bell_draw(key_of[4], (N_REP, SLOTS, BLOCK, BLOCK), 1.0, 6.0, ((0, 48), (2, 16)), jnp.float32)
    left_root = draw_left_root(jax.random.fold_in(key_of[7], 71), 0)
    right_root = draw_right_root(jax.random.fold_in(key_of[7], 71), 0)
    return {"grad_part": grad_part, "owners": owners, "readers": readers, "left_stat": left_stat, "right_stat": right_stat, "left_root": left_root, "right_root": right_root}


decay = 0.95


def precondition(items):
    grad, left_old, right_old, left_factor, right_factor = items
    left_next = decay * left_old + (1.0 - decay) * jnp.dot(grad, grad.T, preferred_element_type=jnp.float32)
    right_next = decay * right_old + (1.0 - decay) * jnp.dot(grad.T, grad, preferred_element_type=jnp.float32)
    mixed = jnp.dot(grad, right_factor, preferred_element_type=jnp.float32).astype(jnp.bfloat16)
    result = jnp.dot(left_factor, mixed, preferred_element_type=jnp.float32).astype(jnp.bfloat16)
    return left_next, right_next, result


def reference(grad_part, owners, readers, left_stat, right_stat, left_root, right_root):
    summed = jnp.sum(grad_part, axis=0)
    blocks = summed.reshape(BLOCK_ROWS, BLOCK, BLOCK_COLS, BLOCK).transpose(0, 2, 1, 3)
    blocks = blocks.reshape(BLOCK_ROWS * BLOCK_COLS, BLOCK, BLOCK).astype(jnp.bfloat16)
    owners_flat = owners.reshape(-1).astype(jnp.int32)
    block_index = jnp.arange(owners_flat.shape[0], dtype=jnp.int32)
    earlier = (owners_flat[:, None] == owners_flat[None, :]) & (block_index[None, :] < block_index[:, None])
    owner_slot = jnp.sum(earlier.astype(jnp.int32), axis=1)
    position = (owners_flat * SLOTS + owner_slot).astype(jnp.int32)
    table = jnp.zeros((N_REP * SLOTS, BLOCK, BLOCK), blocks.dtype).at[position].set(blocks)

    def flatten(array):
        return array.reshape((N_REP * SLOTS, BLOCK, BLOCK))

    left_next, right_next, results = lax.map(
        precondition, (table, flatten(left_stat), flatten(right_stat), flatten(left_root), flatten(right_root)))
    picked = results[position]
    whole = picked.reshape(BLOCK_ROWS, BLOCK_COLS, BLOCK, BLOCK).transpose(0, 2, 1, 3)
    whole = whole.reshape(N_REP, SHARD_ROWS, BLOCK_COLS, BLOCK)
    update = jnp.zeros_like(whole).at[readers.astype(jnp.int32)].set(whole).reshape(ROWS, BLOCK_COLS, BLOCK)
    return update, left_next.reshape(left_stat.shape), right_next.reshape(right_stat.shape)
```

```python
import jax
import jax.numpy as jnp
from jax import lax
from jax.experimental import pallas as pl
from jax.experimental.pallas import tpu as pltpu
from jax.sharding import PartitionSpec as P

MESH = pl.DeviceIdType.MESH
f32 = jnp.float32
bf16 = jnp.bfloat16

decay = 0.95

NX, NZ, NY = 4, 12, 8
N_REP = NX * NZ
COLS = 20
SLOTS = 4
PARTS = 8
NT = (((1,), (1,)), ((), ()))
NN = (((1,), (0,)), ((), ()))
ZERO_PIECE = COLS
ZERO_TILE = N_REP
ZERO_RESULT = SLOTS * PARTS
TAB_B, TAB_C = 0, N_REP
TAB_D = TAB_C + SLOTS * PARTS
TAB_E = TAB_D + N_REP
ORDER = (4, 3, 5, 2, 6, 1, 7, 0)
HALF = COLS // 2


def kernel(
    tab, x_hbm, lstat_hbm, rstat_hbm, lroot_hbm, rroot_hbm,
    upd_ref, lout_ref, rout_ref,
    own, sib, send_a, recv_a, tiles, send_b, recv_b, gath, res, send_d, recv_d, spread,
    lstat, rstat, lroot, rroot,
    own_sem, load_sem, sib_ssem, sib_rsem, a_ssem, a_rsem, b_sem, c_ssem, c_rsem, k_ssem, k_rsem, d_sem,
):
    g = lax.axis_index("grp")
    p = lax.axis_index("rep")
    y = lax.div(g, 2)
    core = lax.rem(g, 2)
    px = lax.div(p, NZ)
    pz = lax.rem(p, NZ)
    sibling = g + 1 - 2 * core
    up = lax.rem(y + 1, NY) * 2 + core
    down = lax.rem(y + NY - 1, NY) * 2 + core

    def peer(n):
        dx = lax.div(n, NZ)
        dz = lax.rem(n, NZ)
        return lax.rem(px + dx, NX) * NZ + lax.rem(pz + dz, NZ)

    def remote(src, dst, ssem, rsem, grp, rep):
        return pltpu.make_async_remote_copy(
            src_ref=src, dst_ref=dst, send_sem=ssem, recv_sem=rsem, device_id=(grp, rep), device_id_type=MESH
        )

    def piece_of(k, who_core):
        there = lax.rem(y + k, NY)
        row = pl.multiple_of(lax.div(there, 2) * 16, 16)
        col = pl.multiple_of((lax.rem(there, 2) * 2 + who_core) * 128, 128)
        return x_hbm.at[0, pl.ds(row, 16), :, pl.ds(col, 128)]

    own_loads = {k: pltpu.make_async_copy(piece_of(k, core), own.at[k], own_sem.at[k]) for k in ORDER}
    for k in ORDER:
        own_loads[k].start()
    late_loads = [
        pltpu.make_async_copy(src, dst, load_sem.at[i])
        for i, (src, dst) in enumerate(
            ((lstat_hbm.at[0], lstat), (rstat_hbm.at[0], rstat), (lroot_hbm.at[0], lroot), (rroot_hbm, rroot))
        )
    ]
    for one in late_loads:
        one.start()

    barrier = pltpu.get_barrier_semaphore()
    for who in (sibling, up, down):
        pl.semaphore_signal(barrier, inc=1, device_id=(who, p), device_id_type=MESH)

    def greet(n, carry):
        pl.semaphore_signal(barrier, inc=1, device_id=(g, peer(n)), device_id_type=MESH)
        return carry

    lax.fori_loop(1, N_REP, greet, 0)
    tiles[ZERO_PIECE] = jnp.zeros((16, 128), bf16)
    recv_b[ZERO_TILE] = jnp.zeros((16, 128), bf16)
    res[ZERO_RESULT] = jnp.zeros((16, 128), bf16)
    pl.semaphore_wait(barrier, N_REP - 1 + 3)

    pair = {
        k: remote(piece_of(k, 1 - core), sib.at[k], sib_ssem.at[k], sib_rsem.at[k], sibling, p) for k in ORDER
    }
    for k in ORDER:
        pair[k].start()

    def pair_sum(k, j):
        return own[k, :, j, :] + sib[k, :, j, :]

    arrived = set()

    def need(k):
        if k not in arrived:
            arrived.add(k)
            own_loads[k].wait()
            pair[k].wait_recv()

    def chain(way, dist, part):
        slot = (way * 4 + dist - 1) * 2 + part
        span = pl.ds(part * HALF, HALF)
        return remote(
            send_a.at[way, dist - 1, span], recv_a.at[way, dist - 1, span],
            a_ssem.at[slot], a_rsem.at[slot], down if way else up, p,
        )

    def send_sum(way, dist, part, from_dist):
        k = NY - dist if way else dist
        need(k)
        if from_dist:
            chain(way, from_dist, part).wait_recv()
        for j in range(part * HALF, part * HALF + HALF):
            total = pair_sum(k, j)
            if from_dist:
                total = total + recv_a[way, from_dist - 1, j].astype(f32)
            send_a[way, dist - 1, j] = total.astype(bf16)
        chain(way, dist, part).start()

    for way in range(2):
        send_sum(way, 4, way, None)
    for way in range(2):
        send_sum(way, 3, 1 - way, None)
    for way in range(2):
        send_sum(way, 3, way, 4)
    for dist in (2, 1):
        for part in range(2):
            for way in range(2):
                send_sum(way, dist, (1 - part) if way == 0 else part, dist + 1)
    need(0)
    for part in range(2):
        for way in range(2):
            chain(way, 1, part).wait_recv()
        for j in range(part * HALF, part * HALF + HALF):
            total = pair_sum(0, j) + recv_a[0, 0, j].astype(f32) + recv_a[1, 0, j].astype(f32)
            tiles[j] = total.astype(bf16)

    recv_b[0] = tiles[tab[TAB_B]]

    def send_piece(n, carry):
        send_b[n] = tiles[tab[TAB_B + n]]
        remote(send_b.at[n], recv_b.at[n], b_sem.at[0], b_sem.at[1], g, peer(n)).start()
        return carry

    lax.fori_loop(1, N_REP, send_piece, 0)
    rest = pl.ds(1, N_REP - 1)
    all_b = remote(send_b.at[rest], recv_b.at[rest], b_sem.at[0], b_sem.at[1], g, p)
    all_b.wait_recv()

    def home(y_of, core_of, s):
        who = y_of * 2 + core_of
        return gath.at[s, lax.rem(who, 4), :, lax.div(who, 4)]

    for s in range(SLOTS):
        for u in range(PARTS):
            gath[s, lax.rem(g, 4), u, lax.div(g, 4)] = recv_b[tab[TAB_C + s * PARTS + u]]

    def ring(way, dist, s, y_of):
        place = home(y_of, core, s)
        index = (way * 4 + dist - 1) * SLOTS + s
        return remote(place, place, c_ssem.at[index], c_rsem.at[index], down if way else up, p)

    def across(index, s, y_of, core_of):
        place = home(y_of, core_of, s)
        return remote(place, place, k_ssem.at[index * SLOTS + s], k_rsem.at[index * SLOTS + s], sibling, p)

    def back(way, dist):
        return lax.rem(y + dist, NY) if way else lax.rem(y + NY - dist, NY)

    def carries(way, dist, s):
        return dist < 4 or (s >= SLOTS // 2) == bool(way)

    def relay(way, dist):
        return way * 4 + dist

    for s in range(SLOTS):
        for way in range(2):
            ring(way, 1, s, y).start()
        across(0, s, y, core).start()
    for dist in range(1, 5):
        for s in range(SLOTS):
            for way in range(2):
                if not carries(way, dist, s):
                    continue
                origin = back(way, dist)
                ring(way, dist, s, origin).wait_recv()
                if dist < 4 and carries(way, dist + 1, s):
                    ring(way, dist + 1, s, origin).start()
                across(relay(way, dist), s, origin, core).start()

    for one in late_loads:
        one.wait()
    lanes = lax.broadcasted_iota(jnp.int32, (32, 512), 1)
    picks = lax.broadcasted_iota(jnp.int32, (32, 512), 0) + g * 32
    pick = jnp.where(lanes == picks, 1.0, 0.0).astype(bf16)
    lane_group = lax.div(lax.broadcasted_iota(jnp.int32, (512, 128), 1), 32)

    for s in range(SLOTS):
        across(0, s, y, 1 - core).wait_recv()
        for way in range(2):
            for dist in range(1, 5):
                if carries(way, dist, s):
                    across(relay(way, dist), s, back(way, dist), 1 - core).wait_recv()

    def products(s, carry):
        whole = jnp.concatenate([gath[s, q].reshape(512, 128) for q in range(4)], axis=1)
        band = pl.ds(lax.rem(g, 2) * 2, 2)
        mine = jnp.concatenate(
            [gath[s, q, lax.div(g, 2), band].reshape(32, 128) for q in range(4)], axis=1
        )
        first = lax.dot_general(jnp.concatenate([mine, pick], axis=0), whole, NT, preferred_element_type=f32)
        lout_ref[0, s] = decay * lstat[s] + (1.0 - decay) * first[:32]
        strip = first[32:].astype(bf16)
        second = lax.dot_general(strip, whole, NN, preferred_element_type=f32)
        rout_ref[0, s] = decay * rstat[s] + (1.0 - decay) * second
        mixed = lax.dot_general(whole, rroot[s], NN, preferred_element_type=f32)
        packed = jnp.zeros((128, 128), f32)
        for q in range(4):
            quarter = jnp.where(lane_group == q, mixed, 0.0).astype(bf16)
            factor = lroot[s, :, q].reshape(128, 512)
            packed = packed + lax.dot_general(factor, quarter, NN, preferred_element_type=f32)
        res[pl.ds(s * PARTS, PARTS)] = packed.astype(bf16).reshape(PARTS, 16, 128)
        return carry

    lax.fori_loop(0, SLOTS, products, 0)

    recv_d[0] = res[tab[TAB_D]]

    def send_rows(n, carry):
        send_d[n] = res[tab[TAB_D + n]]
        remote(send_d.at[n], recv_d.at[n], d_sem.at[0], d_sem.at[1], g, peer(n)).start()
        return carry

    lax.fori_loop(1, N_REP, send_rows, 0)
    all_d = remote(send_d.at[rest], recv_d.at[rest], d_sem.at[0], d_sem.at[1], g, p)
    all_d.wait_recv()

    def unpack(j, carry):
        rows = recv_d[tab[TAB_E + j]].astype(f32)
        for q in range(4):
            spread[j, pl.ds(q * 16, 16), :] = pltpu.roll(rows, (128 - 32 * q) % 128, 1)
        return carry

    lax.fori_loop(0, COLS, unpack, 0)
    for j in range(COLS):
        upd_ref[:, j, :] = spread[j, :, 0:32].astype(bf16)

    for k in ORDER:
        pair[k].wait_send()
    for way in range(2):
        for dist in range(1, 5):
            for part in range(2):
                if dist < 4 or part == way:
                    chain(way, dist, part).wait_send()
    all_b.wait_send()
    for s in range(SLOTS):
        across(0, s, y, core).wait_send()
        for way in range(2):
            for dist in range(1, 5):
                if carries(way, dist, s):
                    ring(way, dist, s, y).wait_send()
                    across(relay(way, dist), s, y, core).wait_send()
    all_d.wait_send()


def tables(owners, readers):
    me = lax.axis_index("rep").astype(jnp.int32)
    mx, mz = me // NZ, me % NZ
    n = jnp.arange(N_REP, dtype=jnp.int32)
    dest = (mx + n // NZ) % NX * NZ + (mz + n % NZ) % NZ

    def rel(src):
        return (mx - src // NZ) % NX * NZ + (mz - src % NZ) % NZ

    cols = jnp.arange(COLS, dtype=jnp.int32)
    targets = lax.dynamic_index_in_dim(owners, me // PARTS, 0, keepdims=False)
    tab_b = jnp.min(jnp.where(targets[None, :] == dest[:, None], cols[None, :], ZERO_PIECE), axis=1)
    has = jnp.any(owners == me, axis=1)
    rows = jnp.arange(owners.shape[0], dtype=jnp.int32)
    slot = jnp.sum((has[None, :] & (rows[None, :] < rows[:, None])).astype(jnp.int32), axis=1)
    slots = jnp.arange(SLOTS, dtype=jnp.int32)
    hit = has[None, :] & (slot[None, :] == slots[:, None])
    row_of = jnp.sum(jnp.where(hit, rows[None, :], 0), axis=1)
    filled = jnp.any(hit, axis=1)
    parts = jnp.arange(PARTS, dtype=jnp.int32)
    tab_c = jnp.where(filled[:, None], rel(row_of[:, None] * PARTS + parts[None, :]), ZERO_TILE)
    source = jnp.sum(jnp.where(readers[None, :] == dest[:, None], n[None, :], 0), axis=1)
    in_row = (source // PARTS)[:, None] == rows[None, :]
    place = jnp.sum(jnp.where(in_row & has[None, :], slot[None, :] + 1, 0), axis=1)
    tab_d = jnp.where(place > 0, (place - 1) * PARTS + source % PARTS, ZERO_RESULT)
    my_source = jnp.sum(jnp.where(readers == me, n, 0))
    row_owners = lax.dynamic_index_in_dim(owners, my_source // PARTS, 0, keepdims=False)
    tab_e = rel(row_owners)
    return jnp.concatenate([tab_b, tab_c.reshape(-1), tab_d, tab_e])


def on_device(grad_part, owners, readers, left_stat, right_stat, left_root, right_root):
    tab = tables(owners, readers)
    roots = left_root.reshape(1, SLOTS, PARTS, 4, 16, 512)
    strips = jnp.tile(right_root[0], (1, 1, 4))
    hbm = pl.BlockSpec(memory_space=pl.ANY)
    vmem = pl.BlockSpec(memory_space=pltpu.VMEM)
    dma = pltpu.SemaphoreType.DMA
    return pl.pallas_call(
        kernel,
        out_shape=(
            jax.ShapeDtypeStruct((64, COLS, 32), bf16),
            jax.ShapeDtypeStruct(left_stat.shape, f32),
            jax.ShapeDtypeStruct(right_stat.shape, f32),
        ),
        in_specs=[pl.BlockSpec(memory_space=pltpu.SMEM)] + [hbm] * 5,
        out_specs=(vmem, vmem, vmem),
        scratch_shapes=[
            pltpu.VMEM((NY, 16, COLS, 128), f32),
            pltpu.VMEM((NY, 16, COLS, 128), f32),
            pltpu.VMEM((2, 4, COLS, 16, 128), bf16),
            pltpu.VMEM((2, 4, COLS, 16, 128), bf16),
            pltpu.VMEM((COLS + 1, 16, 128), bf16),
            pltpu.VMEM((N_REP, 16, 128), bf16),
            pltpu.VMEM((N_REP + 1, 16, 128), bf16),
            pltpu.VMEM((SLOTS, 4, PARTS, 4, 16, 128), bf16),
            pltpu.VMEM((SLOTS * PARTS + 1, 16, 128), bf16),
            pltpu.VMEM((N_REP, 16, 128), bf16),
            pltpu.VMEM((N_REP, 16, 128), bf16),
            pltpu.VMEM((COLS, 64, 128), f32),
            pltpu.VMEM((SLOTS, 32, 512), f32),
            pltpu.VMEM((SLOTS, 32, 512), f32),
            pltpu.VMEM((SLOTS, PARTS, 4, 16, 512), bf16),
            pltpu.VMEM((SLOTS, 512, 128), bf16),
            dma((NY,)), dma((4,)), dma((NY,)), dma((NY,)), dma((16,)), dma((16,)), dma((2,)),
            dma((8 * SLOTS,)), dma((8 * SLOTS,)), dma((9 * SLOTS,)), dma((9 * SLOTS,)), dma((2,)),
        ],
        compiler_params=pltpu.CompilerParams(
            collective_id=0, has_side_effects=True, vmem_limit_bytes=48 * 1024 * 1024
        ),
        cost_estimate=pl.CostEstimate(flops=300_000_000, bytes_accessed=8_000_000, transcendentals=0),
    )(tab, grad_part, left_stat, right_stat, roots, strips)


def solution(mesh):
    placed = (
        P("grp", "rep", None, None),
        P(),
        P(),
        P("rep", None, "grp", None),
        P("rep", None, "grp", None),
        P("rep", None, None, None),
        P("rep", None, None, "grp"),
    )
    return jax.shard_map(
        on_device,
        mesh=mesh,
        in_specs=placed,
        out_specs=(P("rep", None, "grp"), P("rep", None, "grp", None), P("rep", None, "grp", None)),
        check_vma=False,
    )
```

```python
import jax
import jax.numpy as jnp
from jax import lax
from jax.experimental import pallas as pl
from jax.experimental.pallas import tpu as pltpu
from jax.sharding import PartitionSpec as P

MESH = pl.DeviceIdType.MESH
f32 = jnp.float32
bf16 = jnp.bfloat16

decay = 0.95

NX, NZ, NY = 4, 12, 8
N_REP = NX * NZ
BLOCK_ROWS = 6
COLS = 20
SLOTS = 4
PARTS = 8
NT = (((1,), (1,)), ((), ()))
NN = (((1,), (0,)), ((), ()))
ZERO_PIECE = COLS
ZERO_TILE = N_REP
ZERO_RESULT = SLOTS * PARTS
TAB_B, TAB_C, TAB_D, TAB_E = 0, 1, 2, 3
PLANE = [(dx, dz) for i in (5, 4, 3, 2, 1, 0) for dz in (i, NZ - 1 - i) for dx in range(NX) if dx or dz]
HALF = COLS // 2
QUARTER = COLS // 4


def kernel(
    owners, readers, x_hbm, lstat_hbm, rstat_hbm, lroot_hbm, rroot_hbm,
    upd_hbm, lout_hbm, rout_hbm,
    own, sib, send_a, recv_a, tiles, send_b, recv_b, gath, res, send_d, recv_d,
    lstat, rstat, lroot, rroot, lout, rout, upd, tab_v, tab,
    own_sem, load_sem, tab_sem, sib_ssem, sib_rsem, a_ssem, a_rsem, b_sem, c_ssem, c_rsem, k_ssem, k_rsem, d_sem,
    round_sem, out_sem,
):
    g = lax.axis_index("grp")
    p = lax.axis_index("rep")
    y = lax.div(g, 2)
    core = lax.rem(g, 2)
    px = lax.div(p, NZ)
    pz = lax.rem(p, NZ)
    sibling = g + 1 - 2 * core
    up = lax.rem(y + 1, NY) * 2 + core
    down = lax.rem(y + NY - 1, NY) * 2 + core
    at_x = [lax.rem(px + dx, NX) * NZ for dx in range(NX)]
    at_z = [lax.rem(pz + dz, NZ) for dz in range(NZ)]

    def peer(dx, dz):
        return at_x[dx % NX] + at_z[dz % NZ]

    def remote(src, dst, ssem, rsem, grp, rep):
        return pltpu.make_async_remote_copy(
            src_ref=src, dst_ref=dst, send_sem=ssem, recv_sem=rsem, device_id=(grp, rep), device_id_type=MESH
        )

    def rows_of(half, who_core, part):
        row = pl.multiple_of(who_core * 32 + half * 16, 16)
        return x_hbm.at[pl.ds(part * HALF, HALF), pl.ds(row, 16)]

    batches = [(i, half, part) for i, (half, part) in enumerate(((0, 0), (0, 1), (1, 0), (1, 1)))]

    def strip_of(k):
        there = lax.rem(y + k, NY)
        half = lax.div(there, 4)
        cols = pl.ds(pl.multiple_of(lax.rem(there, 4) * 128, 128), 128)
        rows = pl.ds(pl.multiple_of((1 - core) * 32 + half * 16, 16), 16)
        return remote(
            x_hbm.at[:, rows, cols], sib.at[k], sib_ssem.at[k], sib_rsem.at[k], sibling, p
        )

    def band(ref, half, part):
        return ref.at[half, pl.ds(part * HALF, HALF)]

    own_loads = [
        pltpu.make_async_copy(rows_of(half, core, part), band(own, half, part), own_sem.at[i])
        for i, half, part in batches
    ]
    for one in own_loads:
        one.start()

    barrier = pltpu.get_barrier_semaphore()
    for who in (sibling, up, down):
        pl.semaphore_signal(barrier, inc=1, device_id=(who, p), device_id_type=MESH)

    for dx, dz in ((1, 0), (-1, 0), (0, 1), (0, -1)):
        pl.semaphore_signal(barrier, inc=1, device_id=(g, peer(dx, dz)), device_id_type=MESH)
    tiles[ZERO_PIECE] = jnp.zeros((16, 128), bf16)
    recv_b[ZERO_TILE] = jnp.zeros((16, 128), bf16)
    res[ZERO_RESULT] = jnp.zeros((16, 128), bf16)
    pl.semaphore_wait(barrier, 7)

    rounds = (
        ((0, 1), (0, -1)), ((0, 2), (0, -2)), ((0, 2), (0, -2)), ((1, 0), (-1, 0)), ((1, 0),),
    )

    def tell(i):
        for dx, dz in rounds[i]:
            pl.semaphore_signal(round_sem.at[i], inc=1, device_id=(g, peer(dx, dz)), device_id_type=MESH)

    def hear(i):
        pl.semaphore_wait(round_sem.at[i], len(rounds[i]))
        if i + 1 < len(rounds):
            tell(i + 1)

    strip_of(4).start()
    tell(0)
    late_loads = [
        pltpu.make_async_copy(src, dst, load_sem.at[i])
        for i, (src, dst) in enumerate(
            ((lstat_hbm.at[0], lstat), (rstat_hbm.at[0], rstat), (lroot_hbm.at[0], lroot), (rroot_hbm, rroot))
        )
    ]
    for one in late_loads:
        one.start()
    fill_tables(owners, readers, tab_v, p, px, pz)
    tab_copy = pltpu.make_async_copy(tab_v, tab, tab_sem.at[0])
    tab_copy.start()
    strip_of(3).start()
    strip_of(5).start()
    hear(0)
    for one in own_loads:
        one.wait()

    def pair_sum(k, j):
        there = lax.rem(y + k, NY)
        at = (lax.div(there, 4), j, slice(None), pl.ds(pl.multiple_of(lax.rem(there, 4) * 128, 128), 128))
        return own[at] + sib[k, j]

    arrived = set()

    def need(k):
        if k not in arrived:
            arrived.add(k)
            strip_of(k).wait_recv()

    def chain(way, dist, part):
        slot = (way * 4 + dist - 1) * 4 + part
        span = pl.ds(part * QUARTER, QUARTER)
        return remote(
            send_a.at[way, dist - 1, span], recv_a.at[way, dist - 1, span],
            a_ssem.at[slot], a_rsem.at[slot], down if way else up, p,
        )

    def span_of(part):
        return range(part * QUARTER, part * QUARTER + QUARTER)

    def send_sum(way, dist, part, from_dist):
        k = NY - dist if way else dist
        need(k)
        if from_dist:
            chain(way, from_dist, part).wait_recv()
        for j in span_of(part):
            total = pair_sum(k, j)
            if from_dist:
                total = total + recv_a[way, from_dist - 1, j].astype(f32)
            send_a[way, dist - 1, j] = total.astype(bf16)
        chain(way, dist, part).start()

    far_parts = ((0, 1), (2, 3))
    for i in range(2):
        for way in range(2):
            send_sum(way, 4, far_parts[way][i], None)
    strip_of(2).start()
    strip_of(6).start()
    hear(1)
    for i in range(2):
        for way in range(2):
            send_sum(way, 3, far_parts[1 - way][i], None)
    for k in (1, 7, 0):
        strip_of(k).start()
    hear(2)
    for i in range(2):
        for way in range(2):
            send_sum(way, 3, far_parts[way][i], 4)
    for dist in (2, 1):
        hear(5 - dist)
        for i in range(4):
            for way in range(2):
                send_sum(way, dist, (2, 3, 0, 1)[i] if way == 0 else i, dist + 1)
    need(0)
    for part in range(4):
        for way in range(2):
            chain(way, 1, part).wait_recv()
        for j in span_of(part):
            total = pair_sum(0, j) + recv_a[0, 0, j].astype(f32) + recv_a[1, 0, j].astype(f32)
            tiles[j] = total.astype(bf16)

    tab_copy.wait()
    recv_b[0] = tiles[tab[TAB_B, 0]]
    for dx, dz in PLANE:
        n = dx * NZ + dz
        send_b[n] = tiles[tab[TAB_B, n]]
        remote(send_b.at[n], recv_b.at[n], b_sem.at[0], b_sem.at[1], g, peer(dx, dz)).start()
    rest = pl.ds(1, N_REP - 1)
    all_b = remote(send_b.at[rest], recv_b.at[rest], b_sem.at[0], b_sem.at[1], g, p)
    all_b.wait_recv()

    def home(y_of, core_of, s):
        return gath.at[s, lax.rem(y_of, 4), 2 * core_of + lax.div(y_of, 4)]

    for s in range(SLOTS):
        for u in range(PARTS):
            gath[s, lax.rem(y, 4), 2 * core + lax.div(y, 4), u] = recv_b[tab[TAB_C, s * PARTS + u]]

    def ring(way, dist, s, y_of):
        place = home(y_of, core, s)
        index = (way * 4 + dist - 1) * SLOTS + s
        return remote(place, place, c_ssem.at[index], c_rsem.at[index], down if way else up, p)

    def across(index, s, y_of, core_of):
        place = home(y_of, core_of, s)
        return remote(place, place, k_ssem.at[index * SLOTS + s], k_rsem.at[index * SLOTS + s], sibling, p)

    def back(way, dist):
        return lax.rem(y + dist, NY) if way else lax.rem(y + NY - dist, NY)

    def carries(way, dist, s):
        return dist < 4 or s % 2 == way

    def relay(way, dist):
        return way * 4 + dist

    def launch(s):
        for way in range(2):
            ring(way, 1, s, y).start()
        across(0, s, y, core).start()

    def forward(dist, s):
        for way in range(2):
            if carries(way, dist, s):
                origin = back(way, dist)
                ring(way, dist, s, origin).wait_recv()
                if dist < 4 and carries(way, dist + 1, s):
                    ring(way, dist + 1, s, origin).start()
                across(relay(way, dist), s, origin, core).start()

    def gathered(s):
        across(0, s, y, 1 - core).wait_recv()
        for way in range(2):
            for dist in range(1, 5):
                if carries(way, dist, s):
                    across(relay(way, dist), s, back(way, dist), 1 - core).wait_recv()

    left_half = lax.broadcasted_iota(jnp.int32, (16, 128), 1) < 64

    def block_of(s):
        return jnp.concatenate(
            [jnp.concatenate([gath[s, q, h, u] for u in range(PARTS) for h in range(4)], axis=0) for q in range(4)],
            axis=1,
        )

    def precondition(s):
        mixed = lax.dot_general(rroot[s], block_of(s), NT, preferred_element_type=f32).astype(bf16)
        result = lax.dot_general(mixed, lroot[s], NT, preferred_element_type=f32)
        for v in range(PARTS // 2):
            top = result[:16, v * 128 : v * 128 + 128]
            low = result[16:, v * 128 : v * 128 + 128]
            res[s * PARTS + 2 * v] = jnp.where(left_half, top, pltpu.roll(low, 64, 1)).astype(bf16)
            res[s * PARTS + 2 * v + 1] = jnp.where(left_half, pltpu.roll(top, 64, 1), low).astype(bf16)

    groups = ((0, 1), (2, 3))
    for s in groups[0]:
        launch(s)
    for one in late_loads:
        one.wait()
    for s in groups[0]:
        for way in range(2):
            ring(way, 1, s, y).wait_send()
    for s in groups[1]:
        launch(s)
    for dist in range(1, 5):
        for s in range(SLOTS):
            forward(dist, s)
    for s in range(SLOTS):
        gathered(s)
        precondition(s)

    recv_d[0] = res[tab[TAB_D, 0]]
    for dx, dz in PLANE:
        n = dx * NZ + dz
        send_d[n] = res[tab[TAB_D, n]]
        remote(send_d.at[n], recv_d.at[n], d_sem.at[0], d_sem.at[1], g, peer(dx, dz)).start()
    all_d = remote(send_d.at[rest], recv_d.at[rest], d_sem.at[0], d_sem.at[1], g, p)
    lanes = lax.broadcasted_iota(jnp.int32, (32, 512), 1)
    picks = lax.broadcasted_iota(jnp.int32, (32, 512), 0) + g * 32
    pick = jnp.where(lanes == picks, 1.0, 0.0).astype(bf16)
    pair_rows = pl.ds(core * 2, 2)

    def out_copy(src, dst, i):
        return pltpu.make_async_copy(src, dst, out_sem.at[i])

    def out_left(s):
        return out_copy(lout.at[s], lout_hbm.at[0, s], 2 * s)

    def out_right(s):
        return out_copy(rout.at[s], rout_hbm.at[0, s], 2 * s + 1)

    for s in range(SLOTS):
        whole = block_of(s)
        mine = jnp.concatenate([gath[s, q, pair_rows, y].reshape(32, 128) for q in range(4)], axis=1)
        rows = jnp.concatenate([mine, pick], axis=0)
        first = lax.dot_general(rows, whole, NT, preferred_element_type=f32)
        lout[s] = decay * lstat[s] + (1.0 - decay) * first[:32]
        out_left(s).start()
        second = lax.dot_general(first[32:].astype(bf16), whole, NN, preferred_element_type=f32)
        rout[s] = decay * rstat[s] + (1.0 - decay) * second
        out_right(s).start()

    all_d.wait_recv()

    def unpack(j, carry):
        rows = recv_d[tab[TAB_E, j]]
        upd[j, 0:16] = rows[:, 0:64]
        upd[j, 16:32] = pltpu.roll(rows.astype(f32), 64, 1)[:, 0:64].astype(bf16)
        return carry

    lax.fori_loop(0, COLS, unpack, 0, unroll=4)
    out_update = out_copy(upd, upd_hbm, 2 * SLOTS)
    out_update.start()

    for k in range(NY):
        strip_of(k).wait_send()
    for way in range(2):
        for dist in range(1, 5):
            for part in range(4):
                if dist < 4 or part in far_parts[way]:
                    chain(way, dist, part).wait_send()
    all_b.wait_send()
    for s in range(SLOTS):
        across(0, s, y, core).wait_send()
        for way in range(2):
            for dist in range(1, 5):
                if carries(way, dist, s):
                    if dist > 1 or s in groups[1]:
                        ring(way, dist, s, y).wait_send()
                    across(relay(way, dist), s, y, core).wait_send()
    all_d.wait_send()
    for s in range(SLOTS):
        out_left(s).wait()
        out_right(s).wait()
    out_update.wait()


def fill_tables(owners, readers, tab_v, p, px, pz):
    lane = lax.broadcasted_iota(jnp.int32, (1, 128), 1)
    one = jnp.int32(1)
    nil = jnp.int32(0)

    def dozens(v):
        return jnp.where(v >= NZ, one, nil) + jnp.where(v >= 2 * NZ, one, nil) + jnp.where(v >= 3 * NZ, one, nil)

    def rel(src):
        sx = dozens(src)
        dx = px - sx
        dz = pz - (src - NZ * sx)
        return jnp.where(dx < 0, dx + NX, dx) * NZ + jnp.where(dz < 0, dz + NZ, dz)

    hop_x = dozens(lane)
    to_x = px + hop_x
    to_z = pz + lane - NZ * hop_x
    dest = jnp.where(to_x >= NX, to_x - NX, to_x) * NZ + jnp.where(to_z >= NZ, to_z - NZ, to_z)
    my_row = lax.div(p, PARTS)
    piece = jnp.full((1, 128), ZERO_PIECE, jnp.int32)
    for j in range(COLS):
        piece = jnp.where(dest == owners[my_row, j], j, piece)
    tab_v[TAB_B : TAB_B + 1] = piece

    def count(j, held):
        return tuple(jnp.where(owners[i, j] == p, one, h) for i, h in enumerate(held))

    has = lax.fori_loop(0, COLS, count, (nil,) * BLOCK_ROWS)
    slot, total = [], nil
    for i in range(BLOCK_ROWS):
        slot.append(total)
        total = total + has[i]
    row = jnp.zeros((1, 128), jnp.int32)
    filled = jnp.zeros((1, 128), jnp.int32)
    for i in range(BLOCK_ROWS):
        hit = jnp.where(lax.shift_right_logical(lane, 3) == slot[i], has[i], 0)
        row = row + i * hit
        filled = filled + hit
    tab_v[TAB_C : TAB_C + 1] = jnp.where(filled > 0, rel(row * PARTS + (lane & 7)), ZERO_TILE)

    def find(q, carry):
        source, mine = carry
        reader = readers[q]
        return jnp.where(dest == reader, q, source), jnp.where(reader == p, q, mine)

    source, mine = lax.fori_loop(0, N_REP, find, (jnp.zeros((1, 128), jnp.int32), nil))
    source_row = lax.shift_right_logical(source, 3)
    place = jnp.zeros((1, 128), jnp.int32)
    for i in range(BLOCK_ROWS):
        place = place + jnp.where(source_row == i, has[i] * (slot[i] + 1), 0)
    found = jnp.where(place > 0, (place - 1) * PARTS + (source & 7), ZERO_RESULT)
    tab_v[TAB_D : TAB_D + 1] = jnp.minimum(found, ZERO_RESULT)
    mine_row = lax.div(mine, PARTS)
    holder = jnp.zeros((1, 128), jnp.int32)
    for j in range(COLS):
        holder = jnp.where(lane == j, owners[mine_row, j], holder)
    tab_v[TAB_E : TAB_E + 1] = rel(holder)


def hand_over(upd_in, left_in, right_in, upd_out, left_out, right_out):
    upd_out[...] = upd_in[...]
    left_out[...] = left_in[...]
    right_out[...] = right_in[...]


def on_device(grad_part, owners, readers, left_stat, right_stat, left_root, right_root):
    grads = jnp.transpose(grad_part[0], (1, 0, 2))
    strips = jnp.transpose(right_root[0], (0, 2, 1))
    hbm = pl.BlockSpec(memory_space=pl.ANY)
    vmem = pl.BlockSpec(memory_space=pltpu.VMEM)
    dma = pltpu.SemaphoreType.DMA
    update, left_next, right_next = pl.pallas_call(
        kernel,
        out_shape=(
            jax.ShapeDtypeStruct((COLS, 32, 64), bf16),
            jax.ShapeDtypeStruct(left_stat.shape, f32),
            jax.ShapeDtypeStruct(right_stat.shape, f32),
        ),
        in_specs=[pl.BlockSpec(memory_space=pltpu.SMEM)] * 2 + [hbm] * 5,
        out_specs=(hbm, hbm, hbm),
        scratch_shapes=[
            pltpu.VMEM((2, COLS, 16, 512), f32),
            pltpu.VMEM((NY, COLS, 16, 128), f32),
            pltpu.VMEM((2, 4, COLS, 16, 128), bf16),
            pltpu.VMEM((2, 4, COLS, 16, 128), bf16),
            pltpu.VMEM((COLS + 1, 16, 128), bf16),
            pltpu.VMEM((N_REP, 16, 128), bf16),
            pltpu.VMEM((N_REP + 1, 16, 128), bf16),
            pltpu.VMEM((SLOTS, 4, 4, PARTS, 16, 128), bf16),
            pltpu.VMEM((SLOTS * PARTS + 1, 16, 128), bf16),
            pltpu.VMEM((N_REP, 16, 128), bf16),
            pltpu.VMEM((N_REP, 16, 128), bf16),
            pltpu.VMEM((SLOTS, 32, 512), f32),
            pltpu.VMEM((SLOTS, 32, 512), f32),
            pltpu.VMEM((SLOTS, 512, 512), bf16),
            pltpu.VMEM((SLOTS, 32, 512), bf16),
            pltpu.VMEM((SLOTS, 32, 512), f32),
            pltpu.VMEM((SLOTS, 32, 512), f32),
            pltpu.VMEM((COLS, 32, 64), bf16),
            pltpu.VMEM((4, 128), jnp.int32),
            pltpu.SMEM((4, 128), jnp.int32),
            dma((4,)), dma((4,)), dma((1,)), dma((NY,)), dma((NY,)), dma((32,)), dma((32,)), dma((2,)),
            dma((8 * SLOTS,)), dma((8 * SLOTS,)), dma((9 * SLOTS,)), dma((9 * SLOTS,)), dma((2,)),
            pltpu.SemaphoreType.REGULAR((5,)), dma((2 * SLOTS + 1,)),
        ],
        compiler_params=pltpu.CompilerParams(
            collective_id=0, has_side_effects=True, vmem_limit_bytes=60 * 1024 * 1024
        ),
        cost_estimate=pl.CostEstimate(flops=300_000_000, bytes_accessed=8_000_000, transcendentals=0),
    )(owners, readers, grads, left_stat, right_stat, left_root, strips)
    update, left_next, right_next = pl.pallas_call(
        hand_over,
        out_shape=tuple(jax.ShapeDtypeStruct(one.shape, one.dtype) for one in (update, left_next, right_next)),
        in_specs=[vmem] * 3,
        out_specs=(vmem,) * 3,
        compiler_params=pltpu.CompilerParams(vmem_limit_bytes=60 * 1024 * 1024),
    )(update, left_next, right_next)
    return jnp.transpose(update, (2, 0, 1)), left_next, right_next


def solution(mesh):
    placed = (
        P("grp", "rep", None, None),
        P(),
        P(),
        P("rep", None, "grp", None),
        P("rep", None, "grp", None),
        P("rep", None, None, None),
        P("rep", None, None, "grp"),
    )
    return jax.shard_map(
        on_device,
        mesh=mesh,
        in_specs=placed,
        out_specs=(P("rep", None, "grp"), P("rep", None, "grp", None), P("rep", None, "grp", None)),
        check_vma=False,
    )
```

```python
import jax
import jax.numpy as jnp
from jax import lax
from jax.experimental import pallas as pl
from jax.experimental.pallas import tpu as pltpu
from jax.sharding import PartitionSpec as P

MESH = pl.DeviceIdType.MESH
f32 = jnp.float32
bf16 = jnp.bfloat16

decay = 0.95

NX, NZ, NY = 4, 12, 8
N_REP = NX * NZ
BLOCK_ROWS = 6
COLS = 20
SLOTS = 4
PARTS = 8
NT = (((1,), (1,)), ((), ()))
NN = (((1,), (0,)), ((), ()))
ZERO_PIECE = COLS
ZERO_TILE = N_REP
ZERO_RESULT = SLOTS * PARTS
TAB_B, TAB_C, TAB_D, TAB_E = 0, 1, 2, 3
PLANE = [(dx, dz) for i in (5, 4, 3, 2, 1, 0) for dz in (i, NZ - 1 - i) for dx in range(NX) if dx or dz]
HALF = COLS // 2
QUARTER = COLS // 4


def kernel(
    owners, readers, x_hbm, lstat_hbm, rstat_hbm, lroot_hbm, rroot_hbm,
    upd_hbm, lout_hbm, rout_hbm,
    own, sib, send_a, recv_a, tiles, send_b, recv_b, gath, res, send_d, recv_d,
    lstat, rstat, lroot, rroot, lout, rout, upd, tab_v, tab,
    own_sem, load_sem, tab_sem, sib_ssem, sib_rsem, a_ssem, a_rsem, b_sem, c_ssem, c_rsem, k_ssem, k_rsem, d_sem,
    round_sem, out_sem,
):
    g = lax.axis_index("grp")
    p = lax.axis_index("rep")
    y = lax.div(g, 2)
    core = lax.rem(g, 2)
    px = lax.div(p, NZ)
    pz = lax.rem(p, NZ)
    sibling = g + 1 - 2 * core
    up = lax.rem(y + 1, NY) * 2 + core
    down = lax.rem(y + NY - 1, NY) * 2 + core
    up_two = lax.rem(y + 2, NY) * 2 + core
    down_two = lax.rem(y + NY - 2, NY) * 2 + core
    at_x = [lax.rem(px + dx, NX) * NZ for dx in range(NX)]
    at_z = [lax.rem(pz + dz, NZ) for dz in range(NZ)]

    def peer(dx, dz):
        return at_x[dx % NX] + at_z[dz % NZ]

    def along(way, dist):
        if dist == 4:
            return down_two if way else up_two
        return down if way else up

    def remote(src, dst, ssem, rsem, grp, rep):
        return pltpu.make_async_remote_copy(
            src_ref=src, dst_ref=dst, send_sem=ssem, recv_sem=rsem, device_id=(grp, rep), device_id_type=MESH
        )

    def rows_of(half, who_core, part):
        row = pl.multiple_of(who_core * 32 + half * 16, 16)
        return x_hbm.at[pl.ds(part * HALF, HALF), pl.ds(row, 16)]

    batches = [(i, half, part) for i, (half, part) in enumerate(((0, 0), (0, 1), (1, 0), (1, 1)))]

    def strip_of(k):
        there = lax.rem(y + k, NY)
        half = lax.div(there, 4)
        cols = pl.ds(pl.multiple_of(lax.rem(there, 4) * 128, 128), 128)
        rows = pl.ds(pl.multiple_of((1 - core) * 32 + half * 16, 16), 16)
        return remote(
            x_hbm.at[:, rows, cols], sib.at[k], sib_ssem.at[k], sib_rsem.at[k], sibling, p
        )

    def band(ref, half, part):
        return ref.at[half, pl.ds(part * HALF, HALF)]

    own_loads = [
        pltpu.make_async_copy(rows_of(half, core, part), band(own, half, part), own_sem.at[i])
        for i, half, part in batches
    ]
    for one in own_loads:
        one.start()

    barrier = pltpu.get_barrier_semaphore()
    for who in (sibling, up, down, up_two, down_two):
        pl.semaphore_signal(barrier, inc=1, device_id=(who, p), device_id_type=MESH)

    for dx, dz in ((1, 0), (-1, 0), (0, 1), (0, -1)):
        pl.semaphore_signal(barrier, inc=1, device_id=(g, peer(dx, dz)), device_id_type=MESH)
    tiles[ZERO_PIECE] = jnp.zeros((16, 128), bf16)
    recv_b[ZERO_TILE] = jnp.zeros((16, 128), bf16)
    res[ZERO_RESULT] = jnp.zeros((16, 128), bf16)
    pl.semaphore_wait(barrier, 9)

    rounds = (
        ((0, 1), (0, -1)), ((0, 2), (0, -2)), ((0, 2), (0, -2)), ((1, 0), (-1, 0)), ((1, 0),),
    )

    def tell(i):
        for dx, dz in rounds[i]:
            pl.semaphore_signal(round_sem.at[i], inc=1, device_id=(g, peer(dx, dz)), device_id_type=MESH)

    def hear(i):
        pl.semaphore_wait(round_sem.at[i], len(rounds[i]))
        if i + 1 < len(rounds):
            tell(i + 1)

    strip_of(4).start()
    tell(0)
    strip_of(3).start()
    strip_of(5).start()
    hear(0)
    for one in own_loads:
        one.wait()

    def pair_sum(k, j):
        there = lax.rem(y + k, NY)
        at = (lax.div(there, 4), j, slice(None), pl.ds(pl.multiple_of(lax.rem(there, 4) * 128, 128), 128))
        return own[at] + sib[k, j]

    arrived = set()

    def need(k):
        if k not in arrived:
            arrived.add(k)
            strip_of(k).wait_recv()

    def chain(way, dist, part):
        slot = (way * 4 + dist - 1) * 4 + part
        span = pl.ds(part * QUARTER, QUARTER)
        return remote(
            send_a.at[way, dist - 1, span], recv_a.at[way, dist - 1, span],
            a_ssem.at[slot], a_rsem.at[slot], along(way, dist), p,
        )

    def span_of(part):
        return range(part * QUARTER, part * QUARTER + QUARTER)

    def send_sum(way, dist, part, sources):
        k = NY - dist if way else dist
        need(k)
        for source in sources:
            chain(way, source, part).wait_recv()
        for j in span_of(part):
            total = pair_sum(k, j)
            for source in sources:
                total = total + recv_a[way, source - 1, j].astype(f32)
            send_a[way, dist - 1, j] = total.astype(bf16)
        chain(way, dist, part).start()

    far_parts = ((0, 1), (2, 3))
    for i in range(2):
        for way in range(2):
            send_sum(way, 4, far_parts[way][i], ())
    strip_of(2).start()
    strip_of(6).start()
    fill_tables(owners, readers, tab_v, p, px, pz)
    tab_copy = pltpu.make_async_copy(tab_v, tab, tab_sem.at[0])
    tab_copy.start()
    hear(1)
    for i in range(2):
        for way in range(2):
            send_sum(way, 3, far_parts[1 - way][i], ())
    for k in (1, 7, 0):
        strip_of(k).start()
    late_loads = [
        pltpu.make_async_copy(src, dst, load_sem.at[i])
        for i, (src, dst) in enumerate(
            ((lstat_hbm.at[0], lstat), (rstat_hbm.at[0], rstat), (lroot_hbm.at[0], lroot), (rroot_hbm, rroot))
        )
    ]
    for one in late_loads:
        one.start()
    hear(2)
    for i in range(2):
        for way in range(2):
            send_sum(way, 3, far_parts[way][i], ())
    for dist in (2, 1):
        hear(5 - dist)
        for i in range(4):
            for way in range(2):
                part = (2, 3, 0, 1)[i] if way == 0 else i
                far = (4,) if dist == 2 and part in far_parts[way] else ()
                send_sum(way, dist, part, (dist + 1,) + far)
    need(0)
    for part in range(4):
        for way in range(2):
            chain(way, 1, part).wait_recv()
        for j in span_of(part):
            total = pair_sum(0, j) + recv_a[0, 0, j].astype(f32) + recv_a[1, 0, j].astype(f32)
            tiles[j] = total.astype(bf16)

    tab_copy.wait()
    recv_b[0] = tiles[tab[TAB_B, 0]]
    for dx, dz in PLANE:
        n = dx * NZ + dz
        send_b[n] = tiles[tab[TAB_B, n]]
        remote(send_b.at[n], recv_b.at[n], b_sem.at[0], b_sem.at[1], g, peer(dx, dz)).start()
    rest = pl.ds(1, N_REP - 1)
    all_b = remote(send_b.at[rest], recv_b.at[rest], b_sem.at[0], b_sem.at[1], g, p)
    all_b.wait_recv()

    def home(y_of, core_of, s):
        return gath.at[s, lax.rem(y_of, 4), 2 * core_of + lax.div(y_of, 4)]

    for s in range(SLOTS):
        for u in range(PARTS):
            gath[s, lax.rem(y, 4), 2 * core + lax.div(y, 4), u] = recv_b[tab[TAB_C, s * PARTS + u]]

    def ring(way, dist, s, y_of):
        place = home(y_of, core, s)
        index = (way * 4 + dist - 1) * SLOTS + s
        return remote(place, place, c_ssem.at[index], c_rsem.at[index], along(way, dist), p)

    def across(index, s, y_of, core_of):
        place = home(y_of, core_of, s)
        return remote(place, place, k_ssem.at[index * SLOTS + s], k_rsem.at[index * SLOTS + s], sibling, p)

    def back(way, dist):
        return lax.rem(y + dist, NY) if way else lax.rem(y + NY - dist, NY)

    def carries(way, dist, s):
        return dist < 4 or s % 2 == way

    def relay(way, dist):
        return way * 4 + dist

    def launch(s):
        for way in range(2):
            ring(way, 1, s, y).start()
        across(0, s, y, core).start()

    def forward(dist, s):
        for way in range(2):
            if carries(way, dist, s):
                origin = back(way, dist)
                ring(way, dist, s, origin).wait_recv()
                if dist == 2 and carries(way, 4, s):
                    ring(way, 4, s, origin).start()
                if dist < 3:
                    ring(way, dist + 1, s, origin).start()
                across(relay(way, dist), s, origin, core).start()

    def sibling_pieces(dist):
        for s in range(SLOTS):
            if dist == 0:
                across(0, s, y, 1 - core).wait_recv()
                continue
            for way in range(2):
                if carries(way, dist, s):
                    across(relay(way, dist), s, back(way, dist), 1 - core).wait_recv()

    left_half = lax.broadcasted_iota(jnp.int32, (16, 128), 1) < 64

    def block_of(s):
        return jnp.concatenate(
            [jnp.concatenate([gath[s, q, h, u] for u in range(PARTS) for h in range(4)], axis=0) for q in range(4)],
            axis=1,
        )

    def precondition(s):
        mixed = lax.dot_general(rroot[s], block_of(s), NT, preferred_element_type=f32).astype(bf16)
        result = lax.dot_general(mixed, lroot[s], NT, preferred_element_type=f32)
        for v in range(PARTS // 2):
            top = result[:16, v * 128 : v * 128 + 128]
            low = result[16:, v * 128 : v * 128 + 128]
            res[s * PARTS + 2 * v] = jnp.where(left_half, top, pltpu.roll(low, 64, 1)).astype(bf16)
            res[s * PARTS + 2 * v + 1] = jnp.where(left_half, pltpu.roll(top, 64, 1), low).astype(bf16)

    for s in range(SLOTS):
        launch(s)
    for one in late_loads:
        one.wait()
    for dist in range(1, 5):
        for s in range(SLOTS):
            forward(dist, s)
        sibling_pieces(dist - 1)
    sibling_pieces(4)
    for s in range(SLOTS):
        precondition(s)

    recv_d[0] = res[tab[TAB_D, 0]]
    for dx, dz in PLANE:
        n = dx * NZ + dz
        send_d[n] = res[tab[TAB_D, n]]
        remote(send_d.at[n], recv_d.at[n], d_sem.at[0], d_sem.at[1], g, peer(dx, dz)).start()
    all_d = remote(send_d.at[rest], recv_d.at[rest], d_sem.at[0], d_sem.at[1], g, p)
    lanes = lax.broadcasted_iota(jnp.int32, (32, 512), 1)
    picks = lax.broadcasted_iota(jnp.int32, (32, 512), 0) + g * 32
    pick = jnp.where(lanes == picks, 1.0, 0.0).astype(bf16)
    pair_rows = pl.ds(core * 2, 2)

    def out_copy(src, dst, i):
        return pltpu.make_async_copy(src, dst, out_sem.at[i])

    def out_left(s):
        return out_copy(lout.at[s], lout_hbm.at[0, s], 2 * s)

    def out_right(s):
        return out_copy(rout.at[s], rout_hbm.at[0, s], 2 * s + 1)

    for s in range(SLOTS):
        whole = block_of(s)
        mine = jnp.concatenate([gath[s, q, pair_rows, y].reshape(32, 128) for q in range(4)], axis=1)
        rows = jnp.concatenate([mine, pick], axis=0)
        first = lax.dot_general(rows, whole, NT, preferred_element_type=f32)
        lout[s] = decay * lstat[s] + (1.0 - decay) * first[:32]
        out_left(s).start()
        second = lax.dot_general(first[32:].astype(bf16), whole, NN, preferred_element_type=f32)
        rout[s] = decay * rstat[s] + (1.0 - decay) * second
        out_right(s).start()

    for k in range(NY):
        strip_of(k).wait_send()
    for way in range(2):
        for dist in range(1, 5):
            for part in range(4):
                if dist < 4 or part in far_parts[way]:
                    chain(way, dist, part).wait_send()
    all_b.wait_send()
    for s in range(SLOTS):
        across(0, s, y, core).wait_send()
        for way in range(2):
            for dist in range(1, 5):
                if carries(way, dist, s):
                    ring(way, dist, s, y).wait_send()
                    across(relay(way, dist), s, y, core).wait_send()
    for s in range(SLOTS):
        out_left(s).wait()
        out_right(s).wait()
    all_d.wait_recv()

    for j in range(COLS):
        rows = recv_d[tab[TAB_E, j]]
        upd[j, 0:16] = rows[:, 0:64]
        upd[j, 16:32] = pltpu.roll(rows.astype(f32), 64, 1)[:, 0:64].astype(bf16)
    out_update = out_copy(upd, upd_hbm, 2 * SLOTS)
    out_update.start()

    all_d.wait_send()
    out_update.wait()


def fill_tables(owners, readers, tab_v, p, px, pz):
    lane = lax.broadcasted_iota(jnp.int32, (1, 128), 1)
    one = jnp.int32(1)
    nil = jnp.int32(0)

    def dozens(v):
        return jnp.where(v >= NZ, one, nil) + jnp.where(v >= 2 * NZ, one, nil) + jnp.where(v >= 3 * NZ, one, nil)

    def rel(src):
        sx = dozens(src)
        dx = px - sx
        dz = pz - (src - NZ * sx)
        return jnp.where(dx < 0, dx + NX, dx) * NZ + jnp.where(dz < 0, dz + NZ, dz)

    hop_x = dozens(lane)
    to_x = px + hop_x
    to_z = pz + lane - NZ * hop_x
    dest = jnp.where(to_x >= NX, to_x - NX, to_x) * NZ + jnp.where(to_z >= NZ, to_z - NZ, to_z)
    my_row = lax.div(p, PARTS)
    piece = jnp.full((1, 128), ZERO_PIECE, jnp.int32)
    for j in range(COLS):
        piece = jnp.where(dest == owners[my_row, j], j, piece)
    tab_v[TAB_B : TAB_B + 1] = piece

    def count(j, held):
        return tuple(jnp.where(owners[i, j] == p, one, h) for i, h in enumerate(held))

    has = lax.fori_loop(0, COLS, count, (nil,) * BLOCK_ROWS)
    slot, total = [], nil
    for i in range(BLOCK_ROWS):
        slot.append(total)
        total = total + has[i]
    row = jnp.zeros((1, 128), jnp.int32)
    filled = jnp.zeros((1, 128), jnp.int32)
    for i in range(BLOCK_ROWS):
        hit = jnp.where(lax.shift_right_logical(lane, 3) == slot[i], has[i], 0)
        row = row + i * hit
        filled = filled + hit
    tab_v[TAB_C : TAB_C + 1] = jnp.where(filled > 0, rel(row * PARTS + (lane & 7)), ZERO_TILE)

    def find(q, carry):
        source, mine = carry
        reader = readers[q]
        return jnp.where(dest == reader, q, source), jnp.where(reader == p, q, mine)

    source, mine = lax.fori_loop(0, N_REP, find, (jnp.zeros((1, 128), jnp.int32), nil))
    source_row = lax.shift_right_logical(source, 3)
    place = jnp.zeros((1, 128), jnp.int32)
    for i in range(BLOCK_ROWS):
        place = place + jnp.where(source_row == i, has[i] * (slot[i] + 1), 0)
    found = jnp.where(place > 0, (place - 1) * PARTS + (source & 7), ZERO_RESULT)
    tab_v[TAB_D : TAB_D + 1] = jnp.minimum(found, ZERO_RESULT)
    mine_row = lax.div(mine, PARTS)
    holder = jnp.zeros((1, 128), jnp.int32)
    for j in range(COLS):
        holder = jnp.where(lane == j, owners[mine_row, j], holder)
    tab_v[TAB_E : TAB_E + 1] = rel(holder)


def hand_over(left_in, right_in, upd_in, left_out, right_out, upd_out, left, right, upd, in_sem, out_sem):
    steps = []
    for src, mid, dst in ((left_in, left, left_out), (right_in, right, right_out)):
        for half in range(2):
            at = (0, pl.ds(half * 2, 2))
            steps.append((src.at[at], mid.at[at], dst.at[at]))
    steps.append((upd_in, upd, upd_out))
    into = [pltpu.make_async_copy(src, mid, in_sem.at[i]) for i, (src, mid, _) in enumerate(steps)]
    out = [pltpu.make_async_copy(mid, dst, out_sem.at[i]) for i, (_, mid, dst) in enumerate(steps)]
    for one in into:
        one.start()
    for here, there in zip(into, out):
        here.wait()
        there.start()
    for one in out:
        one.wait()


def on_device(grad_part, owners, readers, left_stat, right_stat, left_root, right_root):
    grads = jnp.transpose(grad_part[0], (1, 0, 2))
    strips = jnp.transpose(right_root[0], (0, 2, 1))
    hbm = pl.BlockSpec(memory_space=pl.ANY)
    dma = pltpu.SemaphoreType.DMA
    update, left_next, right_next = pl.pallas_call(
        kernel,
        out_shape=(
            jax.ShapeDtypeStruct((COLS, 32, 64), bf16),
            jax.ShapeDtypeStruct(left_stat.shape, f32),
            jax.ShapeDtypeStruct(right_stat.shape, f32),
        ),
        in_specs=[pl.BlockSpec(memory_space=pltpu.SMEM)] * 2 + [hbm] * 5,
        out_specs=(hbm, hbm, hbm),
        scratch_shapes=[
            pltpu.VMEM((2, COLS, 16, 512), f32),
            pltpu.VMEM((NY, COLS, 16, 128), f32),
            pltpu.VMEM((2, 4, COLS, 16, 128), bf16),
            pltpu.VMEM((2, 4, COLS, 16, 128), bf16),
            pltpu.VMEM((COLS + 1, 16, 128), bf16),
            pltpu.VMEM((N_REP, 16, 128), bf16),
            pltpu.VMEM((N_REP + 1, 16, 128), bf16),
            pltpu.VMEM((SLOTS, 4, 4, PARTS, 16, 128), bf16),
            pltpu.VMEM((SLOTS * PARTS + 1, 16, 128), bf16),
            pltpu.VMEM((N_REP, 16, 128), bf16),
            pltpu.VMEM((N_REP, 16, 128), bf16),
            pltpu.VMEM((SLOTS, 32, 512), f32),
            pltpu.VMEM((SLOTS, 32, 512), f32),
            pltpu.VMEM((SLOTS, 512, 512), bf16),
            pltpu.VMEM((SLOTS, 32, 512), bf16),
            pltpu.VMEM((SLOTS, 32, 512), f32),
            pltpu.VMEM((SLOTS, 32, 512), f32),
            pltpu.VMEM((COLS, 32, 64), bf16),
            pltpu.VMEM((4, 128), jnp.int32),
            pltpu.SMEM((4, 128), jnp.int32),
            dma((4,)), dma((4,)), dma((1,)), dma((NY,)), dma((NY,)), dma((32,)), dma((32,)), dma((2,)),
            dma((8 * SLOTS,)), dma((8 * SLOTS,)), dma((9 * SLOTS,)), dma((9 * SLOTS,)), dma((2,)),
            pltpu.SemaphoreType.REGULAR((5,)), dma((2 * SLOTS + 1,)),
        ],
        compiler_params=pltpu.CompilerParams(
            collective_id=0, has_side_effects=True, vmem_limit_bytes=60 * 1024 * 1024
        ),
        cost_estimate=pl.CostEstimate(flops=300_000_000, bytes_accessed=8_000_000, transcendentals=0),
    )(owners, readers, grads, left_stat, right_stat, left_root, strips)
    results = (left_next, right_next, update)
    left_next, right_next, update = pl.pallas_call(
        hand_over,
        out_shape=tuple(jax.ShapeDtypeStruct(one.shape, one.dtype) for one in results),
        in_specs=[hbm] * 3,
        out_specs=(hbm,) * 3,
        scratch_shapes=[pltpu.VMEM(one.shape, one.dtype) for one in results] + [dma((5,)), dma((5,))],
        compiler_params=pltpu.CompilerParams(vmem_limit_bytes=60 * 1024 * 1024),
    )(*results)
    return jnp.transpose(update, (2, 0, 1)), left_next, right_next


def solution(mesh):
    placed = (
        P("grp", "rep", None, None),
        P(),
        P(),
        P("rep", None, "grp", None),
        P("rep", None, "grp", None),
        P("rep", None, None, None),
        P("rep", None, None, "grp"),
    )
    return jax.shard_map(
        on_device,
        mesh=mesh,
        in_specs=placed,
        out_specs=(P("rep", None, "grp"), P("rep", None, "grp", None), P("rep", None, "grp", None)),
        check_vma=False,
    )
```
